1024 devices in a mesh: tm: 32 (over x_hi, y, core), gx: 8 (over z), gy: 4 (over x_lo).
Axes of the slice: x: 8 (x_hi: 2, x_lo: 4; x = x_hi * 4 + x_lo), y: 8, z: 8, core: 2. Of those that a mesh axis runs over, the one named last changes fastest.
Arguments:
- start_state: float32 [32, 32, 64, 512], P('tm', None, 'gx', 'gy'), may hold values from -6 to 6
- wind_x: float32 [32, 32, 64, 512], P('tm', None, 'gx', 'gy'), may hold values from 0.5 to 0.85
- wind_y: float32 [32, 32, 64, 512], P('tm', None, 'gx', 'gy'), may hold values from 0.03 to 0.09
- diffusivity: float32 [32, 32, 64, 512], P('tm', None, 'gx', 'gy'), may hold values from 0.004 to 0.012
- diff_coef: float32 [32, 64, 512], P(None, 'gx', 'gy'), may hold values from 0.05 to 0.24
- time_weight: float32 [32, 32], replicated, may hold values from -1 to 1
Outputs:
- defect: float32 [32, 32, 64, 512], P('tm', None, 'gx', 'gy')
- mixed_defect: float32 [32, 32, 64, 512], P('tm', None, 'gx', 'gy')
The draws below stay inside these ranges and needn't reach their ends.
All inputs are finite; a program needn't handle non-finite values.
Results may differ from the reference program's by a relative error of at most 0.00012.
Values sent between devices are 32-bit elements; how exact they have to be, the bound alone decides.
A program may use at most 32 MiB of HBM per device.

```python
import jax
import jax.numpy as jnp
from jax import lax

LEV = 32
SECTIONS = 8
PASSES = 4
SUB = 32
NX = 64
NY = 512


def level_of(key, shape, split, smallest, high):
    loudness, own = 1.0, jax.random.fold_in(key, 6)
    for axis_at, parts in split:
        steps = jnp.exp(jax.random.uniform(jax.random.fold_in(own, axis_at), (parts,), jnp.float32, smallest / len(split), high / len(split)))
        loudness = loudness * jnp.repeat(steps, shape[axis_at] // parts).reshape([-1 if axis == axis_at else 1 for axis in range(len(shape))])
    return loudness


def scatter_about(key, dims, width, reach, shards=(), held_as=jnp.bfloat16):
    loudness = level_of(key, dims, shards, -0.22, 0.18) if shards else 1.0
    array = jax.random.normal(key, dims, jnp.float32) * width * loudness
    return jnp.minimum(jnp.maximum(array, -reach), reach).astype(held_as)


def setup_inputs(seed: int = 0) -> dict:
    keys = jax.random.split(jax.random.key(seed), 7)
    start_state = scatter_about(keys[0], (SUB, LEV, NX, NY), 1.0, 6.0, ((0, 32), (2, 8), (3, 4)), jnp.float32)
    wind_x = jnp.clip(0.5 + 0.35000002 * jax.random.uniform(keys[1], (SUB, LEV, NX, NY), jnp.float32) ** level_of(keys[1], (SUB, LEV, NX, NY), ((0, 32), (2, 8), (3, 4)), -0.2, 0.2), 0.5, 0.85)
    wind_y = jnp.clip(0.03 + 0.060000004 * jax.random.uniform(keys[2], (SUB, LEV, NX, NY), jnp.float32) ** level_of(keys[2], (SUB, LEV, NX, NY), ((0, 32), (2, 8), (3, 4)), -0.2, 0.2), 0.03, 0.09)
    diffusivity = jnp.clip(0.004 + 0.0079999999 * jax.random.uniform(keys[3], (SUB, LEV, NX, NY), jnp.float32) ** level_of(keys[3], (SUB, LEV, NX, NY), ((0, 32), (2, 8), (3, 4)), -0.2, 0.2), 0.004, 0.012)
    diff_coef = jnp.clip(0.05 + 0.19 * jax.random.uniform(keys[4], (LEV, NX, NY), jnp.float32) ** level_of(keys[4], (LEV, NX, NY), ((1, 8), (2, 4)), -0.2, 0.2), 0.05, 0.24)
    time_weight = scatter_about(keys[5], (SUB, SUB), SUB ** -0.5, 1.0, (), jnp.float32)
    return dict(start_state=start_state, wind_x=wind_x, wind_y=wind_y, diffusivity=diffusivity, diff_coef=diff_coef, time_weight=time_weight)


def pad_rim(field):
    return jnp.pad(field, ((0, 0), (1, 1), (1, 1)))


def advance(padded, wind_east, wind_north, kappa):
    inner = padded[..., 1:-1, 1:-1]
    west = padded[..., :-2, 1:-1]
    east = padded[..., 2:, 1:-1]
    south = padded[..., 1:-1, :-2]
    north = padded[..., 1:-1, 2:]
    return inner - wind_east * (inner - west) - wind_north * (inner - south) + kappa * (west + east + south + north - 4.0 * inner)


def smooth(padded, kappa):
    inner = padded[..., 1:-1, 1:-1]
    west = padded[..., :-2, 1:-1]
    east = padded[..., 2:, 1:-1]
    south = padded[..., 1:-1, :-2]
    north = padded[..., 1:-1, 2:]
    return inner + kappa * (west + east + south + north - 4.0 * inner)


def reference(start_state, wind_x, wind_y, diffusivity, diff_coef, time_weight):
    def propagate(items):
        state, wind_east, wind_north, kappa = items
        for step in range(SECTIONS):
            state = advance(pad_rim(state), wind_east, wind_north, kappa)
        return state

    end_state = lax.map(propagate, (start_state, wind_x, wind_y, diffusivity))
    previous = jnp.concatenate([jnp.zeros_like(end_state[:1]), end_state[:-1]], axis=0)
    defect = start_state - previous
    blend = defect + jnp.einsum("st,tlxy->slxy", time_weight, defect, precision=lax.Precision.HIGHEST)

    def spread(field):
        for step in range(PASSES):
            field = smooth(pad_rim(field), diff_coef)
        return field

    mixed_defect = lax.map(spread, blend)
    return defect, mixed_defect
```

```python
import functools

import jax
import jax.numpy as jnp
from jax import lax
from jax.experimental import pallas as pl
from jax.experimental.pallas import tpu as pltpu
from jax.sharding import PartitionSpec as P

MESH = pl.DeviceIdType.MESH

LEV = 32
OWN0, OWN1, ROWS = 16, 144, 160
CHUNK = 16
STATE, B, D, K, C = range(5)
DIRS = ((-1, 0), (1, 0), (-1, -1), (-1, 1), (1, -1), (1, 1), (0, -1), (0, 1))


def rolled(v, shift):
    return pltpu.roll(v, shift % 128, 1)


def stencil(src, dst, coefs, first, last, diffuse, held=1):
    lane = lax.broadcasted_iota(jnp.int32, (CHUNK, 128), 1)
    low, high = lane < 32, lane >= 96
    lowest, highest = max(first - 1, held), min(last + 1, 5 - held)

    def body(i, carry):
        row = pl.multiple_of(8 + i * CHUNK, 8)
        here = pl.ds(row, CHUNK)
        v = {p: src[p, here, :] for p in range(lowest, highest + 1)}
        up = {p: rolled(v[p], 32) for p in range(lowest, last + 1)}
        down = {p: rolled(v[p], -32) for p in range(first, highest + 1)}
        for p in range(first, last + 1):
            west = jnp.where(low, up[p - 1], up[p]) if p > lowest else up[p]
            east = jnp.where(high, down[p + 1], down[p]) if p < highest else down[p]
            south = src[p, pl.ds(row - 1, CHUNK), :]
            north = src[p, pl.ds(row + 1, CHUNK), :]
            mid = v[p]
            if diffuse:
                new = mid + coefs[C, p, here, :] * (((west + east) + (south + north)) - 4.0 * mid)
            else:
                new = (
                    mid
                    + coefs[B, p, here, :] * (west - mid)
                    + coefs[D, p, here, :] * (south - mid)
                    + coefs[K, p, here, :] * ((east + north) - (mid + mid))
                )
            dst[p, here, :] = new
        return carry

    lax.fori_loop(0, (ROWS - 16) // CHUNK, body, 0)


def kernel(
    st_hbm, wx_hbm, wy_hbm, kf_hbm, dc_hbm, tw_ref,
    defect_ref, mixed_ref,
    raw, ext, second, ping, pong, rows_s, rows_e, rows_o, rows_n, got_s, got_e, prev, dtmp, fin,
    load_sem, send1, recv1, send2, recv2, send3, recv3,
    a2a_send, a2a_recv, next_send, next_recv, out_sem, all_in,
):
    tm, gx, gy = lax.axis_index("tm"), lax.axis_index("gx"), lax.axis_index("gy")
    ntm, ngx, ngy = lax.axis_size("tm"), lax.axis_size("gx"), lax.axis_size("gy")

    def there(dx, dy):
        ok = None
        for cond in (
            (gx > 0) if dx < 0 else None,
            (gx < ngx - 1) if dx > 0 else None,
            (gy > 0) if dy < 0 else None,
            (gy < ngy - 1) if dy > 0 else None,
        ):
            if cond is not None:
                ok = cond if ok is None else jnp.logical_and(ok, cond)
        return ok

    def neighbour(dx, dy):
        return {"gx": gx + dx, "gy": gy + dy}

    barrier = pltpu.get_barrier_semaphore()
    for dx, dy in DIRS:
        @pl.when(there(dx, dy))
        def _(dx=dx, dy=dy):
            pl.semaphore_signal(barrier, 1, device_id=neighbour(dx, dy), device_id_type=MESH)

    @pl.when(tm > 0)
    def _():
        pl.semaphore_signal(barrier, 1, device_id={"tm": 0}, device_id_type=MESH)

    loads = [
        pltpu.make_async_copy(src, raw.at[i], load_sem.at[i])
        for i, src in enumerate((st_hbm.at[0], wx_hbm.at[0], wy_hbm.at[0], kf_hbm.at[0], dc_hbm))
    ]
    for load in loads:
        load.start()

    for ref in (ext.at[STATE], second, ping, pong):
        for p in range(6):
            ref[p, 0:8, :] = jnp.zeros((8, 128), jnp.float32)
            ref[p, ROWS - 8 : ROWS, :] = jnp.zeros((8, 128), jnp.float32)
    fields = [ext.at[i] for i in range(5)] + [second]
    for cond, planes in ((gx == 0, (0, 1)), (gx == ngx - 1, (4, 5))):
        @pl.when(cond)
        def _(planes=planes):
            for ref in fields:
                for p in planes:
                    ref[p] = jnp.zeros((ROWS, 128), jnp.float32)
    for cond, row in ((gy == 0, 8), (gy == ngy - 1, OWN1)):
        @pl.when(cond)
        def _(row=row):
            for ref in fields:
                for p in range(6):
                    ref[p, row : row + 8, :] = jnp.zeros((8, 128), jnp.float32)
    for x in range(8):
        got_e[x, 0:1, :] = jnp.zeros((1, 128), jnp.float32)

    def own_rows(i, half):
        return [raw[i, :, half * 4 + j, :] for j in range(4)]

    def put(i, half, parts):
        ext[i, 2 + half, OWN0:OWN1, :] = jnp.concatenate(parts, axis=0).T

    loads[0].wait()
    for half in range(2):
        put(STATE, half, own_rows(0, half))
    for i in (1, 2, 3):
        loads[i].wait()
    for half in range(2):
        kf = own_rows(3, half)
        put(K, half, kf)
        put(B, half, [a + b for a, b in zip(own_rows(1, half), kf)])
        put(D, half, [a + b for a, b in zip(own_rows(2, half), kf)])
    loads[4].wait()
    for half in range(2):
        put(C, half, own_rows(4, half))

    def y_slices(dy):
        if dy < 0:
            return pl.ds(OWN0, 8), pl.ds(OWN1, 8)
        if dy > 0:
            return pl.ds(OWN1 - 8, 8), pl.ds(OWN0 - 8, 8)
        return pl.ds(OWN0, 128), pl.ds(OWN0, 128)

    def near(dx):
        return (2, 4) if dx < 0 else (3, 1)

    def far(dx):
        return (3, 5) if dx < 0 else (2, 0)

    def copies_first(n, dx, dy):
        ys, yd = y_slices(dy)
        if dx == 0:
            src, dst = ext.at[:, pl.ds(2, 2), ys, :], ext.at[:, pl.ds(2, 2), yd, :]
        else:
            ps, pd = near(dx)
            arrays = pl.ds(0, 4 if dy == 0 else 5)
            src, dst = ext.at[arrays, ps, ys, :], ext.at[arrays, pd, yd, :]
        return [pltpu.make_async_remote_copy(src, dst, send1.at[n], recv1.at[n], device_id=neighbour(dx, dy), device_id_type=MESH)]

    def copies_later(n, dx, dy):
        if dx == 0:
            return []
        ys, yd = y_slices(dy)
        out = []
        if dy == 0:
            ps, pd = near(dx)
            out.append(pltpu.make_async_remote_copy(
                ext.at[C, ps, ys, :], ext.at[C, pd, yd, :], send2.at[6 + n], recv2.at[6 + n], device_id=neighbour(dx, dy), device_id_type=MESH))
        ps, pd = far(dx)
        out.append(pltpu.make_async_remote_copy(
            ext.at[pl.ds(1, 3), ps, ys, :], ext.at[pl.ds(1, 3), pd, yd, :], send2.at[n], recv2.at[n], device_id=neighbour(dx, dy), device_id_type=MESH))
        return out

    def copies_second(n, dx, dy):
        ys, yd = y_slices(dy)
        pd = 2 - 2 * dx
        return [pltpu.make_async_remote_copy(
            second.at[pl.ds(2, 2), ys, :], second.at[pl.ds(pd, 2), yd, :], send3.at[n], recv3.at[n], device_id=neighbour(dx, dy), device_id_type=MESH)]

    def each(copies, act, opposite=False):
        for n, (dx, dy) in enumerate(DIRS):
            sx, sy = (-dx, -dy) if opposite else (dx, dy)

            @pl.when(there(sx, sy))
            def _(n=n, dx=dx, dy=dy):
                for copy in copies(n, dx, dy):
                    act(copy)

    start = lambda copy: copy.start()
    arrived = lambda copy: copy.wait_recv()
    left = lambda copy: copy.wait_send()

    count = jnp.int32(0)
    for dx, dy in DIRS:
        count = count + jnp.where(there(dx, dy), 1, 0)
    pl.semaphore_wait(barrier, count + jnp.where(tm == 0, ntm - 1, 0))

    each(copies_first, start)
    each(copies_later, start)

    @pl.when(tm == 0)
    def _():
        def tell(i, carry):
            pl.semaphore_signal(all_in, 1, device_id={"tm": i}, device_id_type=MESH)
            return carry

        lax.fori_loop(1, ntm, tell, 0)

    each(copies_first, arrived, opposite=True)

    stencil(ext.at[STATE], ping, ext, 1, 4, False)
    stencil(ping, pong, ext, 1, 4, False)
    stencil(pong, ping, ext, 1, 4, False)
    stencil(ping, pong, ext, 2, 3, False)
    for p in (2, 3):
        second[p, OWN0:OWN1, :] = pong[p, OWN0:OWN1, :]
    each(copies_second, start)

    def offset(k):
        dx, j, c = 1 - k // 16, (k // 2) % 8, 1 - k % 2
        dy = jnp.where(j % 2 == 0, 4 + j // 2, 4 - (j + 1) // 2)
        x, y, core = tm // 16, (tm // 2) % 8, tm % 2
        return ((x + dx) % 2) * 16 + ((y + dy) % 8) * 2 + (core + c) % 2

    def exchange(n, src_of, dst_of_me):
        def send(k, carry):
            other = offset(k)
            pltpu.make_async_remote_copy(
                src_of(other), dst_of_me, a2a_send.at[n], a2a_recv.at[n], device_id={"tm": other}, device_id_type=MESH
            ).start()
            return carry

        lax.fori_loop(0, ntm - 1, send, 0)
        pltpu.make_async_copy(src_of(tm), dst_of_me, a2a_recv.at[n]).start()

    def exchanged(n):
        pltpu.make_async_copy(raw.at[1], raw.at[2], a2a_recv.at[n]).wait()

    def sent(n):
        pltpu.make_async_copy(raw.at[1, pl.ds(0, ntm - 1)], raw.at[2, pl.ds(0, ntm - 1)], a2a_send.at[n]).wait()

    def to_rows(planes, dst):
        for half, plane in enumerate(planes):
            flat = plane.T
            for j in range(4):
                dst[half * 4 + j] = flat[j * LEV : (j + 1) * LEV, :]

    each(copies_later, arrived, opposite=True)
    stencil(ext.at[STATE], ping, ext, 1, 4, True)
    stencil(ping, pong, ext, 1, 4, True)
    stencil(pong, ping, ext, 1, 4, True)
    stencil(ping, pong, ext, 2, 3, True)
    to_rows([pong[p, OWN0:OWN1, :] for p in (2, 3)], rows_s)

    @pl.when(tm > 0)
    def _():
        pl.semaphore_wait(all_in, 1)

    exchange(0, lambda t: rows_s.at[:, t, :], got_s.at[:, tm, :])

    each(copies_second, arrived, opposite=True)
    stencil(second, ping, ext, 0, 5, False, 0)
    stencil(ping, pong, ext, 0, 5, False, 0)
    stencil(pong, ping, ext, 0, 5, False, 0)
    stencil(ping, pong, ext, 1, 4, False, 0)
    for p in (2, 3):
        fin[p - 2] = pong[p, OWN0:OWN1, :]
    stencil(pong, ping, ext, 1, 4, True)
    stencil(ping, pong, ext, 1, 4, True)
    stencil(pong, ping, ext, 1, 4, True)
    stencil(ping, pong, ext, 2, 3, True)
    to_rows([pong[p, OWN0:OWN1, :] for p in (2, 3)], rows_e)
    exchange(1, lambda t: rows_e.at[:, t, :], got_e.at[:, tm + 1, :])

    to_rows([fin[0], fin[1]], rows_n)
    onward = pltpu.make_async_remote_copy(
        rows_n, prev, next_send, next_recv, device_id={"tm": jnp.minimum(tm + 1, ntm - 1)}, device_id_type=MESH
    )

    @pl.when(tm < ntm - 1)
    def _():
        onward.start()

    @pl.when(tm == 0)
    def _():
        prev[...] = jnp.zeros_like(prev)

    exchanged(0)
    exchanged(1)
    weights = tw_ref[...]
    for x in range(8):
        both = got_s[x] - got_e[x, 0:LEV, :]
        rows_o[x] = both + jnp.dot(weights, both, precision=lax.Precision.HIGHEST, preferred_element_type=jnp.float32)
    exchange(2, lambda s: rows_o.at[:, s, :], mixed_ref.at[0, tm])

    @pl.when(tm > 0)
    def _():
        onward.wait_recv()

    for x in range(8):
        dtmp[:, x, :] = raw[0, :, x, :] - prev[x]
    store = pltpu.make_async_copy(dtmp, defect_ref.at[0], out_sem)
    store.start()

    each(copies_first, left)
    each(copies_later, left)
    each(copies_second, left)

    @pl.when(tm < ntm - 1)
    def _():
        onward.wait_send()

    sent(0)
    sent(1)
    store.wait()
    exchanged(2)
    sent(2)


def per_device(start_state, wind_x, wind_y, diffusivity, diff_coef, time_weight):
    f32 = jnp.float32
    any_space = pl.BlockSpec(memory_space=pl.ANY)
    dma = pltpu.SemaphoreType.DMA
    return pl.pallas_call(
        kernel,
        out_shape=(jax.ShapeDtypeStruct(start_state.shape, f32),) * 2,
        in_specs=[any_space] * 5 + [pl.BlockSpec(memory_space=pltpu.VMEM)],
        out_specs=(any_space, any_space),
        scratch_shapes=[
            pltpu.VMEM((5, LEV, 8, 128), f32),
            pltpu.VMEM((5, 6, ROWS, 128), f32),
            pltpu.VMEM((6, ROWS, 128), f32),
            pltpu.VMEM((6, ROWS, 128), f32),
            pltpu.VMEM((6, ROWS, 128), f32),
            pltpu.VMEM((8, LEV, 128), f32),
            pltpu.VMEM((8, LEV, 128), f32),
            pltpu.VMEM((8, LEV, 128), f32),
            pltpu.VMEM((8, LEV, 128), f32),
            pltpu.VMEM((8, LEV, 128), f32),
            pltpu.VMEM((8, LEV + 8, 128), f32),
            pltpu.VMEM((8, LEV, 128), f32),
            pltpu.VMEM((LEV, 8, 128), f32),
            pltpu.VMEM((2, 128, 128), f32),
            dma((5,)),
            dma((8,)), dma((8,)), dma((8,)), dma((8,)), dma((8,)), dma((8,)),
            dma((3,)), dma((3,)),
            dma, dma, dma,
            pltpu.SemaphoreType.REGULAR,
        ],
        compiler_params=pltpu.CompilerParams(
            collective_id=0, has_side_effects=True, vmem_limit_bytes=32 * 1024 * 1024
        ),
    )(start_state, wind_x, wind_y, diffusivity, diff_coef, time_weight)


def solution(mesh):
    split = P("tm", None, "gx", "gy")
    return jax.shard_map(
        per_device,
        mesh=mesh,
        in_specs=(split, split, split, split, P(None, "gx", "gy"), P()),
        out_specs=(split, split),
        check_vma=False,
    )
```

```python
import functools

import jax
import jax.numpy as jnp
from jax import lax
from jax.experimental import pallas as pl
from jax.experimental.pallas import tpu as pltpu
from jax.sharding import PartitionSpec as P

MESH = pl.DeviceIdType.MESH

LEV = 32
OWN0, OWN1, ROWS = 16, 144, 160
CHUNK = 144
STATE, B, D, K, C = range(5)
DIRS = ((-1, 0), (1, 0), (-1, -1), (-1, 1), (1, -1), (1, 1), (0, -1), (0, 1))


def rolled(v, shift):
    return pltpu.roll(v, shift % 128, 1)


def stencil(src, dst, coefs, first, last, diffuse, held=1):
    lane = lax.broadcasted_iota(jnp.int32, (CHUNK, 128), 1)
    low, high = lane < 32, lane >= 96
    lowest, highest = max(first - 1, held), min(last + 1, 5 - held)

    for row in range(8, ROWS - 8, CHUNK):
        here = pl.ds(row, CHUNK)
        v = {p: src[p, here, :] for p in range(lowest, highest + 1)}
        up = {p: rolled(v[p], 32) for p in range(lowest, last + 1)}
        down = {p: rolled(v[p], -32) for p in range(first, highest + 1)}
        for p in range(first, last + 1):
            west = jnp.where(low, up[p - 1], up[p]) if p > lowest else up[p]
            east = jnp.where(high, down[p + 1], down[p]) if p < highest else down[p]
            south = src[p, pl.ds(row - 1, CHUNK), :]
            north = src[p, pl.ds(row + 1, CHUNK), :]
            mid = v[p]
            if diffuse:
                new = mid + coefs[C, p, here, :] * (((west + east) + (south + north)) - 4.0 * mid)
            else:
                new = (
                    mid
                    + coefs[B, p, here, :] * (west - mid)
                    + coefs[D, p, here, :] * (south - mid)
                    + coefs[K, p, here, :] * ((east + north) - (mid + mid))
                )
            dst[p, here, :] = new


def kernel(
    st_hbm, wx_hbm, wy_hbm, kf_hbm, dc_hbm, tw_hbm,
    defect_ref, mixed_ref,
    raw, ext, second, ping, pong, rows_s, rows_e, rows_o, rows_n, got_s, got_e, prev, dtmp, fin, tw_ref,
    load_sem, send1, recv1, send2, recv2, send3, recv3,
    a2a_send, a2a_recv, next_send, next_recv, out_sem, all_in, near_in,
):
    tm, gx, gy = lax.axis_index("tm"), lax.axis_index("gx"), lax.axis_index("gy")
    ntm, ngx, ngy = lax.axis_size("tm"), lax.axis_size("gx"), lax.axis_size("gy")

    def there(dx, dy):
        ok = None
        for cond in (
            (gx > 0) if dx < 0 else None,
            (gx < ngx - 1) if dx > 0 else None,
            (gy > 0) if dy < 0 else None,
            (gy < ngy - 1) if dy > 0 else None,
        ):
            if cond is not None:
                ok = cond if ok is None else jnp.logical_and(ok, cond)
        return ok

    def neighbour(dx, dy):
        return {"gx": gx + dx, "gy": gy + dy}

    def offset(k):
        dx, j, c = 1 - k // 16, (k // 2) % 8, 1 - k % 2
        dy = jnp.where(j % 2 == 0, 4 + j // 2, 4 - (j + 1) // 2)
        x, y, core = tm // 16, (tm // 2) % 8, tm % 2
        return ((x + dx) % 2) * 16 + ((y + dy) % 8) * 2 + (core + c) % 2

    def head_at(x, y):
        odd_x, odd_y = lax.rem(x + 2, 2), lax.rem(y + 2, 2)
        return 2 * odd_x + 1 - odd_y

    barrier = pltpu.get_barrier_semaphore()
    head = head_at(gx, gy)
    is_head = tm == head
    for dx, dy in DIRS:
        @pl.when(jnp.logical_and(there(dx, dy), tm != head_at(gx + dx, gy + dy)))
        def _(dx=dx, dy=dy):
            pl.semaphore_signal(barrier, 1, device_id=neighbour(dx, dy), device_id_type=MESH)

    @pl.when(jnp.logical_not(is_head))
    def _():
        pl.semaphore_signal(barrier, 1, device_id={"tm": head}, device_id_type=MESH)

    loads = [
        pltpu.make_async_copy(src, raw.at[i], load_sem.at[i])
        for i, src in enumerate((st_hbm.at[0], wx_hbm.at[0], wy_hbm.at[0], kf_hbm.at[0], dc_hbm))
    ]
    loads.append(pltpu.make_async_copy(tw_hbm, tw_ref, load_sem.at[5]))
    for load in loads:
        load.start()

    for ref in (ext.at[STATE], second, ping, pong):
        for p in range(6):
            ref[p, 0:8, :] = jnp.zeros((8, 128), jnp.float32)
            ref[p, ROWS - 8 : ROWS, :] = jnp.zeros((8, 128), jnp.float32)
    fields = [ext.at[i] for i in range(5)] + [second]
    for cond, planes in ((gx == 0, (0, 1)), (gx == ngx - 1, (4, 5))):
        @pl.when(cond)
        def _(planes=planes):
            for ref in fields:
                for p in planes:
                    ref[p] = jnp.zeros((ROWS, 128), jnp.float32)
    for cond, row in ((gy == 0, 8), (gy == ngy - 1, OWN1)):
        @pl.when(cond)
        def _(row=row):
            for ref in fields:
                for p in range(6):
                    ref[p, row : row + 8, :] = jnp.zeros((8, 128), jnp.float32)
    for x in range(8):
        got_e[x, 0:1, :] = jnp.zeros((1, 128), jnp.float32)

    def own_rows(i, half):
        return [raw[i, :, half * 4 + j, :] for j in range(4)]

    def put(i, half, parts):
        ext[i, 2 + half, OWN0:OWN1, :] = jnp.concatenate(parts, axis=0).T

    loads[0].wait()
    for half in range(2):
        put(STATE, half, own_rows(0, half))
    for i in (1, 2, 3):
        loads[i].wait()
    for half in range(2):
        kf = own_rows(3, half)
        put(K, half, kf)
        put(B, half, [a + b for a, b in zip(own_rows(1, half), kf)])
        put(D, half, [a + b for a, b in zip(own_rows(2, half), kf)])
    loads[4].wait()
    for half in range(2):
        put(C, half, own_rows(4, half))

    def y_slices(dy):
        if dy < 0:
            return pl.ds(OWN0, 8), pl.ds(OWN1, 8)
        if dy > 0:
            return pl.ds(OWN1 - 8, 8), pl.ds(OWN0 - 8, 8)
        return pl.ds(OWN0, 128), pl.ds(OWN0, 128)

    def near(dx):
        return (2, 4) if dx < 0 else (3, 1)

    def far(dx):
        return (3, 5) if dx < 0 else (2, 0)

    def copies_first(n, dx, dy):
        ys, yd = y_slices(dy)
        if dx == 0:
            src, dst = ext.at[:, pl.ds(2, 2), ys, :], ext.at[:, pl.ds(2, 2), yd, :]
        else:
            ps, pd = near(dx)
            arrays = pl.ds(0, 4 if dy == 0 else 5)
            src, dst = ext.at[arrays, ps, ys, :], ext.at[arrays, pd, yd, :]
        return [pltpu.make_async_remote_copy(src, dst, send1.at[n], recv1.at[n], device_id=neighbour(dx, dy), device_id_type=MESH)]

    def copies_later(n, dx, dy):
        if dx == 0:
            return []
        ys, yd = y_slices(dy)
        out = []
        if dy == 0:
            ps, pd = near(dx)
            out.append(pltpu.make_async_remote_copy(
                ext.at[C, ps, ys, :], ext.at[C, pd, yd, :], send2.at[6 + n], recv2.at[6 + n], device_id=neighbour(dx, dy), device_id_type=MESH))
        ps, pd = far(dx)
        out.append(pltpu.make_async_remote_copy(
            ext.at[pl.ds(1, 3), ps, ys, :], ext.at[pl.ds(1, 3), pd, yd, :], send2.at[n], recv2.at[n], device_id=neighbour(dx, dy), device_id_type=MESH))
        return out

    def copies_second(n, dx, dy):
        ys, yd = y_slices(dy)
        pd = 2 - 2 * dx
        return [pltpu.make_async_remote_copy(
            second.at[pl.ds(2, 2), ys, :], second.at[pl.ds(pd, 2), yd, :], send3.at[n], recv3.at[n], device_id=neighbour(dx, dy), device_id_type=MESH)]

    def each(copies, act, opposite=False):
        for n, (dx, dy) in enumerate(DIRS):
            sx, sy = (-dx, -dy) if opposite else (dx, dy)

            @pl.when(there(sx, sy))
            def _(n=n, dx=dx, dy=dy):
                for copy in copies(n, dx, dy):
                    act(copy)

    start = lambda copy: copy.start()
    arrived = lambda copy: copy.wait_recv()
    left = lambda copy: copy.wait_send()

    count = jnp.int32(0)
    for dx, dy in DIRS:
        count = count + jnp.where(there(dx, dy), 1, 0)

    @pl.when(jnp.logical_not(is_head))
    def _():
        pl.semaphore_wait(barrier, count)
        for dx, dy in DIRS:
            @pl.when(jnp.logical_and(there(dx, dy), tm == head_at(gx + dx, gy + dy)))
            def _(dx=dx, dy=dy):
                pl.semaphore_signal(near_in, 1, device_id=neighbour(dx, dy), device_id_type=MESH)

    @pl.when(is_head)
    def _():
        pl.semaphore_wait(near_in, count)

    each(copies_first, start)
    each(copies_later, start)

    @pl.when(is_head)
    def _():
        pl.semaphore_wait(barrier, ntm - 1)

        def tell(k, carry):
            pl.semaphore_signal(all_in, 1, device_id={"tm": offset(k)}, device_id_type=MESH)
            return carry

        lax.fori_loop(0, ntm - 1, tell, 0)

    each(copies_first, arrived, opposite=True)

    stencil(ext.at[STATE], ping, ext, 1, 4, False)
    stencil(ping, pong, ext, 1, 4, False)
    stencil(pong, ping, ext, 1, 4, False)
    stencil(ping, pong, ext, 2, 3, False)
    for p in (2, 3):
        second[p, OWN0:OWN1, :] = pong[p, OWN0:OWN1, :]
    each(copies_second, start)

    def exchange(n, src_of, dst_of_me):
        def send(k, carry):
            other = offset(k)
            pltpu.make_async_remote_copy(
                src_of(other), dst_of_me, a2a_send.at[n], a2a_recv.at[n], device_id={"tm": other}, device_id_type=MESH
            ).start()
            return carry

        lax.fori_loop(0, ntm - 1, send, 0)
        pltpu.make_async_copy(src_of(tm), dst_of_me, a2a_recv.at[n]).start()

    def exchanged(n):
        pltpu.make_async_copy(raw.at[1], raw.at[2], a2a_recv.at[n]).wait()

    def sent(n):
        pltpu.make_async_copy(raw.at[1, pl.ds(0, ntm - 1)], raw.at[2, pl.ds(0, ntm - 1)], a2a_send.at[n]).wait()

    def to_rows(planes, dst):
        for half, plane in enumerate(planes):
            flat = plane.T
            for j in range(4):
                dst[half * 4 + j] = flat[j * LEV : (j + 1) * LEV, :]

    each(copies_later, arrived, opposite=True)
    stencil(ext.at[STATE], ping, ext, 1, 4, True)
    stencil(ping, pong, ext, 1, 4, True)
    stencil(pong, ping, ext, 1, 4, True)
    stencil(ping, pong, ext, 2, 3, True)
    to_rows([pong[p, OWN0:OWN1, :] for p in (2, 3)], rows_s)

    @pl.when(jnp.logical_not(is_head))
    def _():
        pl.semaphore_wait(all_in, 1)

    exchange(0, lambda t: rows_s.at[:, t, :], got_s.at[:, tm, :])

    each(copies_second, arrived, opposite=True)
    stencil(second, ping, ext, 0, 5, False, 0)
    stencil(ping, pong, ext, 0, 5, False, 0)
    stencil(pong, ping, ext, 0, 5, False, 0)
    stencil(ping, pong, ext, 1, 4, False, 0)
    for p in (2, 3):
        fin[p - 2] = pong[p, OWN0:OWN1, :]
    stencil(pong, ping, ext, 1, 4, True)
    stencil(ping, pong, ext, 1, 4, True)
    stencil(pong, ping, ext, 1, 4, True)
    stencil(ping, pong, ext, 2, 3, True)
    to_rows([pong[p, OWN0:OWN1, :] for p in (2, 3)], rows_e)
    exchange(1, lambda t: rows_e.at[:, t, :], got_e.at[:, tm + 1, :])

    to_rows([fin[0], fin[1]], rows_n)
    onward = pltpu.make_async_remote_copy(
        rows_n, prev, next_send, next_recv, device_id={"tm": jnp.minimum(tm + 1, ntm - 1)}, device_id_type=MESH
    )

    @pl.when(tm < ntm - 1)
    def _():
        onward.start()

    @pl.when(tm == 0)
    def _():
        prev[...] = jnp.zeros_like(prev)

    exchanged(0)
    exchanged(1)
    loads[5].wait()
    weights = tw_ref[...]
    for x in range(8):
        both = got_s[x] - got_e[x, 0:LEV, :]
        rows_o[x] = both + jnp.dot(weights, both, precision=lax.Precision.HIGHEST, preferred_element_type=jnp.float32)
    exchange(2, lambda s: rows_o.at[:, s, :], mixed_ref.at[0, tm])

    @pl.when(tm > 0)
    def _():
        onward.wait_recv()

    for x in range(8):
        dtmp[:, x, :] = raw[0, :, x, :] - prev[x]
    store = pltpu.make_async_copy(dtmp, defect_ref.at[0], out_sem)
    store.start()

    each(copies_first, left)
    each(copies_later, left)
    each(copies_second, left)

    @pl.when(tm < ntm - 1)
    def _():
        onward.wait_send()

    sent(0)
    sent(1)
    store.wait()
    exchanged(2)
    sent(2)


def hand_out(a_ref, b_ref, a_out, b_out, held, load_sem, store_sem):
    parts = [(k, src, dst, pl.ds(16 * h, 16)) for h in range(2) for k, (src, dst) in enumerate(((a_ref, a_out), (b_ref, b_out)))]
    loads = [pltpu.make_async_copy(src.at[0, p], held.at[k, p], load_sem.at[n]) for n, (k, src, dst, p) in enumerate(parts)]
    stores = [pltpu.make_async_copy(held.at[k, p], dst.at[0, p], store_sem.at[n]) for n, (k, src, dst, p) in enumerate(parts)]
    for load in loads:
        load.start()
    for load, store in zip(loads, stores):
        load.wait()
        store.start()
    for store in stores:
        store.wait()


def per_device(start_state, wind_x, wind_y, diffusivity, diff_coef, time_weight):
    f32 = jnp.float32
    any_space = pl.BlockSpec(memory_space=pltpu.HBM)
    dma = pltpu.SemaphoreType.DMA
    outs = pl.pallas_call(
        kernel,
        out_shape=(jax.ShapeDtypeStruct(start_state.shape, f32),) * 2,
        in_specs=[any_space] * 6,
        out_specs=(any_space, any_space),
        scratch_shapes=[
            pltpu.VMEM((5, LEV, 8, 128), f32),
            pltpu.VMEM((5, 6, ROWS, 128), f32),
            pltpu.VMEM((6, ROWS, 128), f32),
            pltpu.VMEM((6, ROWS, 128), f32),
            pltpu.VMEM((6, ROWS, 128), f32),
            pltpu.VMEM((8, LEV, 128), f32),
            pltpu.VMEM((8, LEV, 128), f32),
            pltpu.VMEM((8, LEV, 128), f32),
            pltpu.VMEM((8, LEV, 128), f32),
            pltpu.VMEM((8, LEV, 128), f32),
            pltpu.VMEM((8, LEV + 8, 128), f32),
            pltpu.VMEM((8, LEV, 128), f32),
            pltpu.VMEM((LEV, 8, 128), f32),
            pltpu.VMEM((2, 128, 128), f32),
            pltpu.VMEM((LEV, LEV), f32),
            dma((6,)),
            dma((8,)), dma((8,)), dma((8,)), dma((8,)), dma((8,)), dma((8,)),
            dma((3,)), dma((3,)),
            dma, dma, dma,
            pltpu.SemaphoreType.REGULAR, pltpu.SemaphoreType.REGULAR,
        ],
        compiler_params=pltpu.CompilerParams(
            collective_id=0, has_side_effects=True, vmem_limit_bytes=62 * 1024 * 1024
        ),
    )(start_state, wind_x, wind_y, diffusivity, diff_coef, time_weight)
    return pl.pallas_call(
        hand_out,
        out_shape=(jax.ShapeDtypeStruct(start_state.shape, f32),) * 2,
        in_specs=[any_space] * 2,
        out_specs=(any_space, any_space),
        scratch_shapes=[pltpu.VMEM((2, LEV, 8, 128), f32), dma((4,)), dma((4,))],
    )(*outs)


def solution(mesh):
    split = P("tm", None, "gx", "gy")
    return jax.shard_map(
        per_device,
        mesh=mesh,
        in_specs=(split, split, split, split, P(None, "gx", "gy"), P()),
        out_specs=(split, split),
        check_vma=False,
    )
```

```python
import functools

import jax
import jax.numpy as jnp
from jax import lax
from jax.experimental import pallas as pl
from jax.experimental.pallas import tpu as pltpu
from jax.sharding import PartitionSpec as P

MESH = pl.DeviceIdType.MESH

LEV = 32
OWN0, OWN1, ROWS = 16, 144, 160
CHUNK = 144
STATE, B, D, K, C = range(5)
DIRS = ((-1, 0), (1, 0), (-1, -1), (-1, 1), (1, -1), (1, 1), (0, -1), (0, 1))


def rolled(v, shift):
    return pltpu.roll(v, shift % 128, 1)


def stencil(src, dst, coefs, first, last, diffuse, held=1):
    lane = lax.broadcasted_iota(jnp.int32, (CHUNK, 128), 1)
    low, high = lane < 32, lane >= 96
    lowest, highest = max(first - 1, held), min(last + 1, 5 - held)

    for row in range(8, ROWS - 8, CHUNK):
        here = pl.ds(row, CHUNK)
        v = {p: src[p, here, :] for p in range(lowest, highest + 1)}
        up = {p: rolled(v[p], 32) for p in range(lowest, last + 1)}
        down = {p: rolled(v[p], -32) for p in range(first, highest + 1)}
        for p in range(first, last + 1):
            west = jnp.where(low, up[p - 1], up[p]) if p > lowest else up[p]
            east = jnp.where(high, down[p + 1], down[p]) if p < highest else down[p]
            south = src[p, pl.ds(row - 1, CHUNK), :]
            north = src[p, pl.ds(row + 1, CHUNK), :]
            mid = v[p]
            if diffuse:
                new = mid + coefs[C, p, here, :] * (((west + east) + (south + north)) - 4.0 * mid)
            else:
                new = (
                    mid
                    + coefs[B, p, here, :] * (west - mid)
                    + coefs[D, p, here, :] * (south - mid)
                    + coefs[K, p, here, :] * ((east + north) - (mid + mid))
                )
            dst[p, here, :] = new


def kernel(
    st_hbm, wx_hbm, wy_hbm, kf_hbm, dc_hbm, tw_hbm,
    defect_ref, mixed_ref,
    raw, ext, second, ping, pong, rows_s, rows_e, rows_o, rows_n, got_s, got_e, prev, dtmp, fin, tw_ref,
    load_sem, send1, recv1, send2, recv2, send3, recv3,
    a2a_send, a2a_recv, next_send, next_recv, out_sem, all_in, near_in,
):
    tm, gx, gy = lax.axis_index("tm"), lax.axis_index("gx"), lax.axis_index("gy")
    ntm, ngx, ngy = lax.axis_size("tm"), lax.axis_size("gx"), lax.axis_size("gy")

    def there(dx, dy):
        ok = None
        for cond in (
            (gx > 0) if dx < 0 else None,
            (gx < ngx - 1) if dx > 0 else None,
            (gy > 0) if dy < 0 else None,
            (gy < ngy - 1) if dy > 0 else None,
        ):
            if cond is not None:
                ok = cond if ok is None else jnp.logical_and(ok, cond)
        return ok

    def neighbour(dx, dy):
        return {"gx": gx + dx, "gy": gy + dy}

    def offset(k):
        dx, j, c = 1 - k // 16, (k // 2) % 8, 1 - k % 2
        dy = (4 + j // 2 if j % 2 == 0 else 4 - (j + 1) // 2) if isinstance(k, int) else jnp.where(lax.rem(j, 2) == 0, 4 + j // 2, 4 - (j + 1) // 2)
        y, core = lax.rem(lax.div(tm, 2), 8), lax.rem(tm, 2)
        base = tm - 2 * y - core
        return (base if isinstance(dx, int) and dx == 0 else lax.rem(base + 16 * dx, 32)) + 2 * lax.rem(y + dy, 8) + lax.rem(core + c, 2)

    def head_at(x, y):
        odd_x, odd_y = lax.rem(x + 2, 2), lax.rem(y + 2, 2)
        return 2 * odd_x + 1 - odd_y

    barrier = pltpu.get_barrier_semaphore()
    head = head_at(gx, gy)
    is_head = tm == head
    for dx, dy in DIRS:
        @pl.when(jnp.logical_and(there(dx, dy), tm != head_at(gx + dx, gy + dy)))
        def _(dx=dx, dy=dy):
            pl.semaphore_signal(barrier, 1, device_id=neighbour(dx, dy), device_id_type=MESH)

    @pl.when(jnp.logical_not(is_head))
    def _():
        pl.semaphore_signal(barrier, 1, device_id={"tm": head}, device_id_type=MESH)

    loads = [
        pltpu.make_async_copy(src, raw.at[i], load_sem.at[i])
        for i, src in enumerate((st_hbm.at[0], wx_hbm.at[0], wy_hbm.at[0], kf_hbm.at[0], dc_hbm))
    ]
    loads.append(pltpu.make_async_copy(tw_hbm, tw_ref, load_sem.at[5]))
    for load in loads:
        load.start()

    for ref in (ext.at[STATE], second, ping, pong):
        for p in range(6):
            ref[p, 0:8, :] = jnp.zeros((8, 128), jnp.float32)
            ref[p, ROWS - 8 : ROWS, :] = jnp.zeros((8, 128), jnp.float32)
    fields = [ext.at[i] for i in range(5)] + [second]
    for cond, planes in ((gx == 0, (0, 1)), (gx == ngx - 1, (4, 5))):
        @pl.when(cond)
        def _(planes=planes):
            for ref in fields:
                for p in planes:
                    ref[p] = jnp.zeros((ROWS, 128), jnp.float32)
    for cond, row in ((gy == 0, 8), (gy == ngy - 1, OWN1)):
        @pl.when(cond)
        def _(row=row):
            for ref in fields:
                for p in range(6):
                    ref[p, row : row + 8, :] = jnp.zeros((8, 128), jnp.float32)
    for x in range(8):
        got_e[x, 0:1, :] = jnp.zeros((1, 128), jnp.float32)

    def own_rows(i, half):
        return [raw[i, :, half * 4 + j, :] for j in range(4)]

    def put(i, half, parts):
        ext[i, 2 + half, OWN0:OWN1, :] = jnp.concatenate(parts, axis=0).T

    loads[0].wait()
    for half in range(2):
        put(STATE, half, own_rows(0, half))
    for i in (1, 2, 3):
        loads[i].wait()
    for half in range(2):
        kf = own_rows(3, half)
        put(K, half, kf)
        put(B, half, [a + b for a, b in zip(own_rows(1, half), kf)])
        put(D, half, [a + b for a, b in zip(own_rows(2, half), kf)])
    loads[4].wait()
    for half in range(2):
        put(C, half, own_rows(4, half))

    def y_slices(dy):
        if dy < 0:
            return pl.ds(OWN0, 8), pl.ds(OWN1, 8)
        if dy > 0:
            return pl.ds(OWN1 - 8, 8), pl.ds(OWN0 - 8, 8)
        return pl.ds(OWN0, 128), pl.ds(OWN0, 128)

    def near(dx):
        return (2, 4) if dx < 0 else (3, 1)

    def far(dx):
        return (3, 5) if dx < 0 else (2, 0)

    def copies_first(n, dx, dy):
        ys, yd = y_slices(dy)
        if dx == 0:
            src, dst = ext.at[:, pl.ds(2, 2), ys, :], ext.at[:, pl.ds(2, 2), yd, :]
        else:
            ps, pd = near(dx)
            arrays = pl.ds(0, 4 if dy == 0 else 5)
            src, dst = ext.at[arrays, ps, ys, :], ext.at[arrays, pd, yd, :]
        return [pltpu.make_async_remote_copy(src, dst, send1.at[n], recv1.at[n], device_id=neighbour(dx, dy), device_id_type=MESH)]

    def copies_later(n, dx, dy):
        if dx == 0:
            return []
        ys, yd = y_slices(dy)
        out = []
        if dy == 0:
            ps, pd = near(dx)
            out.append(pltpu.make_async_remote_copy(
                ext.at[C, ps, ys, :], ext.at[C, pd, yd, :], send2.at[6 + n], recv2.at[6 + n], device_id=neighbour(dx, dy), device_id_type=MESH))
        ps, pd = far(dx)
        out.append(pltpu.make_async_remote_copy(
            ext.at[pl.ds(1, 3), ps, ys, :], ext.at[pl.ds(1, 3), pd, yd, :], send2.at[n], recv2.at[n], device_id=neighbour(dx, dy), device_id_type=MESH))
        return out

    def copies_second(n, dx, dy):
        ys, yd = y_slices(dy)
        pd = 2 - 2 * dx
        return [pltpu.make_async_remote_copy(
            second.at[pl.ds(2, 2), ys, :], second.at[pl.ds(pd, 2), yd, :], send3.at[n], recv3.at[n], device_id=neighbour(dx, dy), device_id_type=MESH)]

    def each(copies, act, opposite=False):
        for n, (dx, dy) in enumerate(DIRS):
            sx, sy = (-dx, -dy) if opposite else (dx, dy)

            @pl.when(there(sx, sy))
            def _(n=n, dx=dx, dy=dy):
                for copy in copies(n, dx, dy):
                    act(copy)

    start = lambda copy: copy.start()
    arrived = lambda copy: copy.wait_recv()
    left = lambda copy: copy.wait_send()

    count = jnp.int32(0)
    for dx, dy in DIRS:
        count = count + jnp.where(there(dx, dy), 1, 0)

    @pl.when(jnp.logical_not(is_head))
    def _():
        pl.semaphore_wait(barrier, count)
        for dx, dy in DIRS:
            @pl.when(jnp.logical_and(there(dx, dy), tm == head_at(gx + dx, gy + dy)))
            def _(dx=dx, dy=dy):
                pl.semaphore_signal(near_in, 1, device_id=neighbour(dx, dy), device_id_type=MESH)

    @pl.when(is_head)
    def _():
        pl.semaphore_wait(near_in, count)

    each(copies_first, start)
    each(copies_later, start)

    @pl.when(is_head)
    def _():
        pl.semaphore_wait(barrier, ntm - 1)

        def tell(k, carry):
            pl.semaphore_signal(all_in, 1, device_id={"tm": offset(k)}, device_id_type=MESH)
            return carry

        lax.fori_loop(0, ntm - 1, tell, 0)

    each(copies_first, arrived, opposite=True)

    stencil(ext.at[STATE], ping, ext, 1, 4, False)
    stencil(ping, pong, ext, 1, 4, False)
    stencil(pong, ping, ext, 1, 4, False)
    stencil(ping, pong, ext, 2, 3, False)
    for p in (2, 3):
        second[p, OWN0:OWN1, :] = pong[p, OWN0:OWN1, :]
    each(copies_second, start)

    def exchange(n, src_of, dst_of_me):
        def send(k, carry):
            other = offset(k)
            pltpu.make_async_remote_copy(
                src_of(other), dst_of_me, a2a_send.at[n], a2a_recv.at[n], device_id={"tm": other}, device_id_type=MESH
            ).start()
            return carry

        for k in range(ntm - 1):
            send(k, 0)
        pltpu.make_async_copy(src_of(tm), dst_of_me, a2a_recv.at[n]).start()

    def exchanged(n):
        pltpu.make_async_copy(raw.at[1], raw.at[2], a2a_recv.at[n]).wait()

    def sent(n):
        pltpu.make_async_copy(raw.at[1, pl.ds(0, ntm - 1)], raw.at[2, pl.ds(0, ntm - 1)], a2a_send.at[n]).wait()

    def to_rows(planes, dst):
        for half, plane in enumerate(planes):
            flat = plane.T
            for j in range(4):
                dst[half * 4 + j] = flat[j * LEV : (j + 1) * LEV, :]

    each(copies_later, arrived, opposite=True)
    stencil(ext.at[STATE], ping, ext, 1, 4, True)
    stencil(ping, pong, ext, 1, 4, True)
    stencil(pong, ping, ext, 1, 4, True)
    stencil(ping, pong, ext, 2, 3, True)
    to_rows([pong[p, OWN0:OWN1, :] for p in (2, 3)], rows_s)

    @pl.when(jnp.logical_not(is_head))
    def _():
        pl.semaphore_wait(all_in, 1)

    exchange(0, lambda t: rows_s.at[:, t, :], got_s.at[:, tm, :])

    each(copies_second, arrived, opposite=True)
    stencil(second, ping, ext, 0, 5, False, 0)
    stencil(ping, pong, ext, 0, 5, False, 0)
    stencil(pong, ping, ext, 0, 5, False, 0)
    stencil(ping, pong, ext, 1, 4, False, 0)
    for p in (2, 3):
        fin[p - 2] = pong[p, OWN0:OWN1, :]
    stencil(pong, ping, ext, 1, 4, True)
    stencil(ping, pong, ext, 1, 4, True)
    stencil(pong, ping, ext, 1, 4, True)
    stencil(ping, pong, ext, 2, 3, True)
    to_rows([pong[p, OWN0:OWN1, :] for p in (2, 3)], rows_e)
    exchange(1, lambda t: rows_e.at[:, t, :], got_e.at[:, tm + 1, :])

    to_rows([fin[0], fin[1]], rows_n)
    onward = pltpu.make_async_remote_copy(
        rows_n, prev, next_send, next_recv, device_id={"tm": jnp.minimum(tm + 1, ntm - 1)}, device_id_type=MESH
    )

    @pl.when(tm < ntm - 1)
    def _():
        onward.start()

    @pl.when(tm == 0)
    def _():
        prev[...] = jnp.zeros_like(prev)

    exchanged(0)
    exchanged(1)
    loads[5].wait()
    weights = tw_ref[...]
    for x in range(8):
        both = got_s[x] - got_e[x, 0:LEV, :]
        rows_o[x] = both + jnp.dot(weights, both, precision=lax.Precision.HIGHEST, preferred_element_type=jnp.float32)
    exchange(2, lambda s: rows_o.at[:, s, :], mixed_ref.at[0, tm])

    @pl.when(tm > 0)
    def _():
        onward.wait_recv()

    for x in range(8):
        dtmp[:, x, :] = raw[0, :, x, :] - prev[x]
    store = pltpu.make_async_copy(dtmp, defect_ref.at[0], out_sem)
    store.start()

    each(copies_first, left)
    each(copies_later, left)
    each(copies_second, left)

    @pl.when(tm < ntm - 1)
    def _():
        onward.wait_send()

    sent(0)
    sent(1)
    store.wait()
    exchanged(2)
    sent(2)


def hand_out(a_ref, b_ref, a_out, b_out, held, load_sem, store_sem):
    parts = [(k, src, dst, pl.ds(16 * h, 16)) for h in range(2) for k, (src, dst) in enumerate(((a_ref, a_out), (b_ref, b_out)))]
    loads = [pltpu.make_async_copy(src.at[0, p], held.at[k, p], load_sem.at[n]) for n, (k, src, dst, p) in enumerate(parts)]
    stores = [pltpu.make_async_copy(held.at[k, p], dst.at[0, p], store_sem.at[n]) for n, (k, src, dst, p) in enumerate(parts)]
    for load in loads:
        load.start()
    for load, store in zip(loads, stores):
        load.wait()
        store.start()
    for store in stores:
        store.wait()


def per_device(start_state, wind_x, wind_y, diffusivity, diff_coef, time_weight):
    f32 = jnp.float32
    any_space = pl.BlockSpec(memory_space=pltpu.HBM)
    dma = pltpu.SemaphoreType.DMA
    outs = pl.pallas_call(
        kernel,
        out_shape=(jax.ShapeDtypeStruct(start_state.shape, f32),) * 2,
        in_specs=[any_space] * 6,
        out_specs=(any_space, any_space),
        scratch_shapes=[
            pltpu.VMEM((5, LEV, 8, 128), f32),
            pltpu.VMEM((5, 6, ROWS, 128), f32),
            pltpu.VMEM((6, ROWS, 128), f32),
            pltpu.VMEM((6, ROWS, 128), f32),
            pltpu.VMEM((6, ROWS, 128), f32),
            pltpu.VMEM((8, LEV, 128), f32),
            pltpu.VMEM((8, LEV, 128), f32),
            pltpu.VMEM((8, LEV, 128), f32),
            pltpu.VMEM((8, LEV, 128), f32),
            pltpu.VMEM((8, LEV, 128), f32),
            pltpu.VMEM((8, LEV + 8, 128), f32),
            pltpu.VMEM((8, LEV, 128), f32),
            pltpu.VMEM((LEV, 8, 128), f32),
            pltpu.VMEM((2, 128, 128), f32),
            pltpu.VMEM((LEV, LEV), f32),
            dma((6,)),
            dma((8,)), dma((8,)), dma((8,)), dma((8,)), dma((8,)), dma((8,)),
            dma((3,)), dma((3,)),
            dma, dma, dma,
            pltpu.SemaphoreType.REGULAR, pltpu.SemaphoreType.REGULAR,
        ],
        compiler_params=pltpu.CompilerParams(
            collective_id=0, has_side_effects=True, vmem_limit_bytes=62 * 1024 * 1024
        ),
    )(start_state, wind_x, wind_y, diffusivity, diff_coef, time_weight)
    return pl.pallas_call(
        hand_out,
        out_shape=(jax.ShapeDtypeStruct(start_state.shape, f32),) * 2,
        in_specs=[any_space] * 2,
        out_specs=(any_space, any_space),
        scratch_shapes=[pltpu.VMEM((2, LEV, 8, 128), f32), dma((4,)), dma((4,))],
    )(*outs)


def solution(mesh):
    split = P("tm", None, "gx", "gy")
    return jax.shard_map(
        per_device,
        mesh=mesh,
        in_specs=(split, split, split, split, P(None, "gx", "gy"), P()),
        out_specs=(split, split),
        check_vma=False,
    )
```

```python
import functools

import jax
import jax.numpy as jnp
from jax import lax
from jax.experimental import pallas as pl
from jax.experimental.pallas import tpu as pltpu
from jax.sharding import PartitionSpec as P

MESH = pl.DeviceIdType.MESH

LEV = 32
OWN0, OWN1, ROWS = 16, 144, 160
CHUNK = 144
STATE, B, D, K, C = range(5)
DIRS = ((-1, 0), (1, 0), (-1, -1), (-1, 1), (1, -1), (1, 1), (0, -1), (0, 1))


def rolled(v, shift):
    return pltpu.roll(v, shift % 128, 1)


def stencil(src, dst, coefs, first, last, diffuse, held=1):
    lane = lax.broadcasted_iota(jnp.int32, (CHUNK, 128), 1)
    low, high = lane < 32, lane >= 96
    lowest, highest = max(first - 1, held), min(last + 1, 5 - held)

    for row in range(8, ROWS - 8, CHUNK):
        here = pl.ds(row, CHUNK)
        v = {p: src[p, here, :] for p in range(lowest, highest + 1)}
        up = {p: rolled(v[p], 32) for p in range(lowest, last + 1)}
        down = {p: rolled(v[p], -32) for p in range(first, highest + 1)}
        for p in range(first, last + 1):
            west = jnp.where(low, up[p - 1], up[p]) if p > lowest else up[p]
            east = jnp.where(high, down[p + 1], down[p]) if p < highest else down[p]
            south = src[p, pl.ds(row - 1, CHUNK), :]
            north = src[p, pl.ds(row + 1, CHUNK), :]
            mid = v[p]
            if diffuse:
                new = mid + coefs[C, p, here, :] * (((west + east) + (south + north)) - 4.0 * mid)
            else:
                new = (
                    mid
                    + coefs[B, p, here, :] * (west - mid)
                    + coefs[D, p, here, :] * (south - mid)
                    + coefs[K, p, here, :] * ((east + north) - (mid + mid))
                )
            dst[p, here, :] = new


def kernel(
    st_hbm, wx_hbm, wy_hbm, kf_hbm, dc_hbm, tw_hbm,
    defect_ref, mixed_ref,
    raw, ext, second, ping, pong, rows_s, rows_e, rows_o, rows_n, got_s, got_e, prev, dtmp, fin, tw_ref,
    load_sem, send1, recv1, send2, recv2, send3, recv3,
    a2a_send, a2a_recv, next_send, next_recv, out_sem, all_in, near_in,
):
    tm, gx, gy = lax.axis_index("tm"), lax.axis_index("gx"), lax.axis_index("gy")
    ntm, ngx, ngy = lax.axis_size("tm"), lax.axis_size("gx"), lax.axis_size("gy")

    def there(dx, dy):
        ok = None
        for cond in (
            (gx > 0) if dx < 0 else None,
            (gx < ngx - 1) if dx > 0 else None,
            (gy > 0) if dy < 0 else None,
            (gy < ngy - 1) if dy > 0 else None,
        ):
            if cond is not None:
                ok = cond if ok is None else jnp.logical_and(ok, cond)
        return ok

    def neighbour(dx, dy):
        return {"gx": gx + dx, "gy": gy + dy}

    def offset(k):
        dx, j, c = 1 - k // 16, (k // 2) % 8, 1 - k % 2
        dy = (4 + j // 2 if j % 2 == 0 else 4 - (j + 1) // 2) if isinstance(k, int) else jnp.where(lax.rem(j, 2) == 0, 4 + j // 2, 4 - (j + 1) // 2)
        y, core = lax.rem(lax.div(tm, 2), 8), lax.rem(tm, 2)
        base = tm - 2 * y - core
        return (base if isinstance(dx, int) and dx == 0 else lax.rem(base + 16 * dx, 32)) + 2 * lax.rem(y + dy, 8) + lax.rem(core + c, 2)

    def head_at(x, y):
        odd_x, odd_y = lax.rem(x + 2, 2), lax.rem(y + 2, 2)
        return 2 * odd_x + 1 - odd_y

    barrier = pltpu.get_barrier_semaphore()
    head = head_at(gx, gy)
    is_head = tm == head
    for dx, dy in DIRS:
        @pl.when(jnp.logical_and(there(dx, dy), tm != head_at(gx + dx, gy + dy)))
        def _(dx=dx, dy=dy):
            pl.semaphore_signal(barrier, 1, device_id=neighbour(dx, dy), device_id_type=MESH)

    @pl.when(jnp.logical_not(is_head))
    def _():
        pl.semaphore_signal(barrier, 1, device_id={"tm": head}, device_id_type=MESH)

    loads = [
        pltpu.make_async_copy(src, raw.at[i], load_sem.at[i])
        for i, src in enumerate((st_hbm.at[0], wx_hbm.at[0], wy_hbm.at[0], kf_hbm.at[0], dc_hbm))
    ]
    loads.append(pltpu.make_async_copy(tw_hbm, tw_ref, load_sem.at[5]))
    for load in loads:
        load.start()

    for ref in (ext.at[STATE], second, ping, pong):
        for p in range(6):
            ref[p, 0:8, :] = jnp.zeros((8, 128), jnp.float32)
            ref[p, ROWS - 8 : ROWS, :] = jnp.zeros((8, 128), jnp.float32)
    fields = [ext.at[i] for i in range(5)] + [second]
    for cond, planes in ((gx == 0, (0, 1)), (gx == ngx - 1, (4, 5))):
        @pl.when(cond)
        def _(planes=planes):
            for ref in fields:
                for p in planes:
                    ref[p] = jnp.zeros((ROWS, 128), jnp.float32)
    for cond, row in ((gy == 0, 8), (gy == ngy - 1, OWN1)):
        @pl.when(cond)
        def _(row=row):
            for ref in fields:
                for p in range(6):
                    ref[p, row : row + 8, :] = jnp.zeros((8, 128), jnp.float32)
    for x in range(8):
        got_e[x, 0:1, :] = jnp.zeros((1, 128), jnp.float32)

    def own_rows(i, half):
        return [raw[i, :, half * 4 + j, :] for j in range(4)]

    def put(i, half, parts):
        ext[i, 2 + half, OWN0:OWN1, :] = jnp.concatenate(parts, axis=0).T

    loads[0].wait()
    for half in range(2):
        put(STATE, half, own_rows(0, half))
    for i in (1, 2, 3):
        loads[i].wait()
    for half in range(2):
        kf = own_rows(3, half)
        put(K, half, kf)
        put(B, half, [a + b for a, b in zip(own_rows(1, half), kf)])
        put(D, half, [a + b for a, b in zip(own_rows(2, half), kf)])
    def y_slices(dy):
        if dy < 0:
            return pl.ds(OWN0, 8), pl.ds(OWN1, 8)
        if dy > 0:
            return pl.ds(OWN1 - 8, 8), pl.ds(OWN0 - 8, 8)
        return pl.ds(OWN0, 128), pl.ds(OWN0, 128)

    def near(dx):
        return (2, 4) if dx < 0 else (3, 1)

    def far(dx):
        return (3, 5) if dx < 0 else (2, 0)

    def copies_first(n, dx, dy):
        ys, yd = y_slices(dy)
        if dx == 0:
            src, dst = ext.at[pl.ds(0, 4), pl.ds(2, 2), ys, :], ext.at[pl.ds(0, 4), pl.ds(2, 2), yd, :]
        else:
            ps, pd = near(dx)
            arrays = pl.ds(0, 4)
            src, dst = ext.at[arrays, ps, ys, :], ext.at[arrays, pd, yd, :]
        return [pltpu.make_async_remote_copy(src, dst, send1.at[n], recv1.at[n], device_id=neighbour(dx, dy), device_id_type=MESH)]

    def copies_later(n, dx, dy):
        ys, yd = y_slices(dy)
        where = neighbour(dx, dy)
        if dx == 0:
            ps, pd = pl.ds(2, 2), pl.ds(2, 2)
        else:
            ps, pd = near(dx)
        out = [pltpu.make_async_remote_copy(
            ext.at[C, ps, ys, :], ext.at[C, pd, yd, :], send2.at[8 + n], recv2.at[8 + n], device_id=where, device_id_type=MESH)]
        if dx != 0:
            ps, pd = far(dx)
            out.append(pltpu.make_async_remote_copy(
                ext.at[pl.ds(1, 3), ps, ys, :], ext.at[pl.ds(1, 3), pd, yd, :], send2.at[n], recv2.at[n], device_id=where, device_id_type=MESH))
        return out

    def copies_second(n, dx, dy):
        ys, yd = y_slices(dy)
        pd = 2 - 2 * dx
        return [pltpu.make_async_remote_copy(
            second.at[pl.ds(2, 2), ys, :], second.at[pl.ds(pd, 2), yd, :], send3.at[n], recv3.at[n], device_id=neighbour(dx, dy), device_id_type=MESH)]

    def each(copies, act, opposite=False):
        for n, (dx, dy) in enumerate(DIRS):
            sx, sy = (-dx, -dy) if opposite else (dx, dy)

            @pl.when(there(sx, sy))
            def _(n=n, dx=dx, dy=dy):
                for copy in copies(n, dx, dy):
                    act(copy)

    start = lambda copy: copy.start()
    arrived = lambda copy: copy.wait_recv()
    left = lambda copy: copy.wait_send()

    count = jnp.int32(0)
    for dx, dy in DIRS:
        count = count + jnp.where(there(dx, dy), 1, 0)

    @pl.when(jnp.logical_not(is_head))
    def _():
        pl.semaphore_wait(barrier, count)
        for dx, dy in DIRS:
            @pl.when(jnp.logical_and(there(dx, dy), tm == head_at(gx + dx, gy + dy)))
            def _(dx=dx, dy=dy):
                pl.semaphore_signal(near_in, 1, device_id=neighbour(dx, dy), device_id_type=MESH)

    @pl.when(is_head)
    def _():
        pl.semaphore_wait(near_in, count)

    each(copies_first, start)
    loads[4].wait()
    for half in range(2):
        put(C, half, own_rows(4, half))
    each(copies_later, start)

    @pl.when(is_head)
    def _():
        pl.semaphore_wait(barrier, ntm - 1)

        def tell(k, carry):
            pl.semaphore_signal(all_in, 1, device_id={"tm": offset(k)}, device_id_type=MESH)
            return carry

        lax.fori_loop(0, ntm - 1, tell, 0)

    each(copies_first, arrived, opposite=True)

    stencil(ext.at[STATE], ping, ext, 1, 4, False)
    stencil(ping, pong, ext, 1, 4, False)
    stencil(pong, ping, ext, 1, 4, False)
    stencil(ping, pong, ext, 2, 3, False)
    for p in (2, 3):
        second[p, OWN0:OWN1, :] = pong[p, OWN0:OWN1, :]
    each(copies_second, start)

    def exchange(n, src_of, dst_of_me):
        def send(k, carry):
            other = offset(k)
            pltpu.make_async_remote_copy(
                src_of(other), dst_of_me, a2a_send.at[n], a2a_recv.at[n], device_id={"tm": other}, device_id_type=MESH
            ).start()
            return carry

        for k in range(ntm - 1):
            send(k, 0)
        pltpu.make_async_copy(src_of(tm), dst_of_me, a2a_recv.at[n]).start()

    def exchanged(n):
        pltpu.make_async_copy(raw.at[1], raw.at[2], a2a_recv.at[n]).wait()

    def sent(n):
        pltpu.make_async_copy(raw.at[1, pl.ds(0, ntm - 1)], raw.at[2, pl.ds(0, ntm - 1)], a2a_send.at[n]).wait()

    def to_rows(planes, dst):
        for half, plane in enumerate(planes):
            flat = plane.T
            for j in range(4):
                dst[half * 4 + j] = flat[j * LEV : (j + 1) * LEV, :]

    each(copies_later, arrived, opposite=True)
    stencil(ext.at[STATE], ping, ext, 1, 4, True)
    stencil(ping, pong, ext, 1, 4, True)
    stencil(pong, ping, ext, 1, 4, True)
    stencil(ping, pong, ext, 2, 3, True)
    to_rows([pong[p, OWN0:OWN1, :] for p in (2, 3)], rows_s)

    @pl.when(jnp.logical_not(is_head))
    def _():
        pl.semaphore_wait(all_in, 1)

    exchange(0, lambda t: rows_s.at[:, t, :], got_s.at[:, tm, :])

    each(copies_second, arrived, opposite=True)
    stencil(second, ping, ext, 0, 5, False, 0)
    stencil(ping, pong, ext, 0, 5, False, 0)
    stencil(pong, ping, ext, 0, 5, False, 0)
    stencil(ping, pong, ext, 1, 4, False, 0)
    for p in (2, 3):
        fin[p - 2] = pong[p, OWN0:OWN1, :]
    stencil(pong, ping, ext, 1, 4, True)
    stencil(ping, pong, ext, 1, 4, True)
    stencil(pong, ping, ext, 1, 4, True)
    stencil(ping, pong, ext, 2, 3, True)
    to_rows([pong[p, OWN0:OWN1, :] for p in (2, 3)], rows_e)
    exchange(1, lambda t: rows_e.at[:, t, :], got_e.at[:, tm + 1, :])

    to_rows([fin[0], fin[1]], rows_n)
    onward = pltpu.make_async_remote_copy(
        rows_n, prev, next_send, next_recv, device_id={"tm": jnp.minimum(tm + 1, ntm - 1)}, device_id_type=MESH
    )

    @pl.when(tm < ntm - 1)
    def _():
        onward.start()

    @pl.when(tm == 0)
    def _():
        prev[...] = jnp.zeros_like(prev)

    exchanged(0)
    exchanged(1)
    loads[5].wait()
    weights = tw_ref[...]
    for x in range(8):
        both = got_s[x] - got_e[x, 0:LEV, :]
        rows_o[x] = both + jnp.dot(weights, both, precision=lax.Precision.HIGHEST, preferred_element_type=jnp.float32)
    exchange(2, lambda s: rows_o.at[:, s, :], mixed_ref.at[0, tm])

    @pl.when(tm > 0)
    def _():
        onward.wait_recv()

    for x in range(8):
        dtmp[:, x, :] = raw[0, :, x, :] - prev[x]
    store = pltpu.make_async_copy(dtmp, defect_ref.at[0], out_sem)
    store.start()

    each(copies_first, left)
    each(copies_later, left)
    each(copies_second, left)

    @pl.when(tm < ntm - 1)
    def _():
        onward.wait_send()

    sent(0)
    sent(1)
    store.wait()
    exchanged(2)
    sent(2)


def hand_out(a_ref, b_ref, a_out, b_out, held, load_sem, store_sem):
    parts = [(k, src, dst, pl.ds(16 * h, 16)) for h in range(2) for k, (src, dst) in enumerate(((a_ref, a_out), (b_ref, b_out)))]
    loads = [pltpu.make_async_copy(src.at[0, p], held.at[k, p], load_sem.at[n]) for n, (k, src, dst, p) in enumerate(parts)]
    stores = [pltpu.make_async_copy(held.at[k, p], dst.at[0, p], store_sem.at[n]) for n, (k, src, dst, p) in enumerate(parts)]
    for load in loads:
        load.start()
    for load, store in zip(loads, stores):
        load.wait()
        store.start()
    for store in stores:
        store.wait()


def per_device(start_state, wind_x, wind_y, diffusivity, diff_coef, time_weight):
    f32 = jnp.float32
    any_space = pl.BlockSpec(memory_space=pltpu.HBM)
    dma = pltpu.SemaphoreType.DMA
    outs = pl.pallas_call(
        kernel,
        out_shape=(jax.ShapeDtypeStruct(start_state.shape, f32),) * 2,
        in_specs=[any_space] * 6,
        out_specs=(any_space, any_space),
        scratch_shapes=[
            pltpu.VMEM((5, LEV, 8, 128), f32),
            pltpu.VMEM((5, 6, ROWS, 128), f32),
            pltpu.VMEM((6, ROWS, 128), f32),
            pltpu.VMEM((6, ROWS, 128), f32),
            pltpu.VMEM((6, ROWS, 128), f32),
            pltpu.VMEM((8, LEV, 128), f32),
            pltpu.VMEM((8, LEV, 128), f32),
            pltpu.VMEM((8, LEV, 128), f32),
            pltpu.VMEM((8, LEV, 128), f32),
            pltpu.VMEM((8, LEV, 128), f32),
            pltpu.VMEM((8, LEV + 8, 128), f32),
            pltpu.VMEM((8, LEV, 128), f32),
            pltpu.VMEM((LEV, 8, 128), f32),
            pltpu.VMEM((2, 128, 128), f32),
            pltpu.VMEM((LEV, LEV), f32),
            dma((6,)),
            dma((8,)), dma((8,)), dma((16,)), dma((16,)), dma((8,)), dma((8,)),
            dma((3,)), dma((3,)),
            dma, dma, dma,
            pltpu.SemaphoreType.REGULAR, pltpu.SemaphoreType.REGULAR,
        ],
        compiler_params=pltpu.CompilerParams(
            collective_id=0, has_side_effects=True, vmem_limit_bytes=62 * 1024 * 1024
        ),
    )(start_state, wind_x, wind_y, diffusivity, diff_coef, time_weight)
    return pl.pallas_call(
        hand_out,
        out_shape=(jax.ShapeDtypeStruct(start_state.shape, f32),) * 2,
        in_specs=[any_space] * 2,
        out_specs=(any_space, any_space),
        scratch_shapes=[pltpu.VMEM((2, LEV, 8, 128), f32), dma((4,)), dma((4,))],
    )(*outs)


def solution(mesh):
    split = P("tm", None, "gx", "gy")
    return jax.shard_map(
        per_device,
        mesh=mesh,
        in_specs=(split, split, split, split, P(None, "gx", "gy"), P()),
        out_specs=(split, split),
        check_vma=False,
    )
```
